32 devices in a mesh: row: 8 (over y, x, core), col: 4 (over z).
Axes of the slice: x: 2, y: 2, z: 4, core: 2. Of those that a mesh axis runs over, the one named last changes fastest.
Arguments:
- blocks: float32 [8, 4, 288, 4096], P('row', 'col')
- block_slot: int32 [8, 4, 288], P('row', 'col'), may hold values from 0 to 73727, as said below
- sign_vec: int32 [98304], P(('col', 'row')), may hold values from -1 to 1, as said below
Outputs:
- normed_image: float32 [98304, 64], P(('col', 'row'))
- power_image: float32 [98304, 64], P(('col', 'row'))
The draws below stay inside these ranges and needn't reach their ends.
Inputs may be any that keep to these rules, and one draw needn't show every extreme that they name: `block_slot`: each entry is i * 192 + j for a local block row i and block column j; the entries of one device are distinct, and each device names slot 0 and the last slot. `sign_vec`: every entry is -1 or 1.
All inputs are finite; a program needn't handle non-finite values.
Results may differ from the reference program's by a relative error of at most 0.0001.
Values sent between devices are 32-bit elements; how exact they have to be, the bound alone decides.
A program may use at most 128 MiB of HBM per device.

```python
import jax
import jax.numpy as jnp
from jax import lax

ORDER = 98304
BLOCK = 64
PROBES = 64
BLK_DEV = 288
LOCAL = 3072
ROWB = 384
COLB = 192
FAN = 384
N_ROW = 8
N_COL = 4


def draw_blocks(key, part):
    shape_full = (N_ROW, N_COL, BLK_DEV, BLOCK * BLOCK)
    key_vals = jax.random.fold_in(key, 11)
    key_scale = jax.random.fold_in(key, 12)
    values = jax.random.normal(key_vals, shape_full, jnp.float32)
    scales = jnp.exp(jax.random.uniform(key_scale, (N_ROW, N_COL, BLK_DEV, 1), jnp.float32, -1.2, 1.1))
    return values * scales / jnp.sqrt(jnp.float32(FAN))


def draw_block_slot(key, part):
    slot_count = ROWB * COLB
    device_keys = jax.random.split(jax.random.fold_in(key, 21), N_ROW * N_COL)

    def one_device(device_key):
        inner = jax.random.permutation(device_key, slot_count - 2)[:BLK_DEV - 2] + 1
        first = jnp.zeros((1,), jnp.int32)
        final = jnp.full((1,), slot_count - 1, jnp.int32)
        return jnp.concatenate([first, inner.astype(jnp.int32), final])
    return jax.vmap(one_device)(device_keys).reshape(N_ROW, N_COL, BLK_DEV).astype(jnp.int32)


def draw_sign_vec(key, part):
    coins = jax.random.randint(jax.random.fold_in(key, 31), (ORDER,), 0, 2)
    return (2 * coins - 1).astype(jnp.int32)


def setup_inputs(seed: int = 0) -> dict:
    seeds = jax.random.split(jax.random.key(seed), 4)
    blocks = draw_blocks(jax.random.fold_in(seeds[3], 71), 0)
    block_slot = draw_block_slot(jax.random.fold_in(seeds[3], 71), 0)
    sign_vec = draw_sign_vec(jax.random.fold_in(seeds[3], 71), 0)
    return {"blocks": blocks, "block_slot": block_slot, "sign_vec": sign_vec}


def hadamard_sign(row_ids, probe_count):
    low_bits = row_ids % 128
    probe_ids = jnp.arange(probe_count, dtype=jnp.int32)
    parity = jnp.zeros((row_ids.shape[0], probe_count), jnp.int32)
    for bit_pos in range(7):
        left_bit = jnp.bitwise_and(jnp.right_shift(low_bits, bit_pos), 1)
        right_bit = jnp.bitwise_and(jnp.right_shift(probe_ids, bit_pos), 1)
        parity = parity + left_bit[:, None] * right_bit[None, :]
    return (1 - 2 * (parity % 2)).astype(jnp.float32)

def apply_blocks(field, tile_set, targets, sources, transpose):
    field_blocks = field.reshape(ORDER // BLOCK, BLOCK, PROBES)
    pattern_text = 'cbji,cbjk->cbik' if transpose else 'cbij,cbjk->cbik'

    def one_band(total, inputs):
        tiles_now, target_now, source_now = inputs
        picked = field_blocks[source_now]
        contrib = jnp.einsum(pattern_text, tiles_now, picked, precision=lax.Precision.HIGHEST)
        return (total.at[target_now].add(contrib), None)
    start_total = jnp.zeros((ORDER // BLOCK, BLOCK, PROBES), jnp.float32)
    total, _ = lax.scan(one_band, start_total, (tile_set, targets, sources))
    return total.reshape(ORDER, PROBES)

def reference(blocks, block_slot, sign_vec):
    per_piece = LOCAL // BLOCK
    row_grid = jnp.arange(N_ROW, dtype=jnp.int32)[:, None, None]
    col_grid = jnp.arange(N_COL, dtype=jnp.int32)[None, :, None]
    blk_row = block_slot // COLB
    blk_col = block_slot % COLB
    global_row = (col_grid * ROWB + blk_row).astype(jnp.int32)
    global_col = (blk_col // per_piece * ROWB + row_grid * per_piece + blk_col % per_piece).astype(jnp.int32)
    probe = sign_vec.astype(jnp.float32)[:, None] * hadamard_sign(jnp.arange(ORDER, dtype=jnp.int32), PROBES)
    tile_set = blocks.reshape(N_ROW, N_COL, BLK_DEV, BLOCK, BLOCK)
    first_image = apply_blocks(probe, tile_set, global_row, global_col, False)
    col_sums = lax.optimization_barrier(jnp.sum(first_image * first_image, axis=0))
    normed_image = first_image / jnp.sqrt(col_sums / ORDER + 1e-06)
    power_image = apply_blocks(normed_image, tile_set, global_col, global_row, True)
    return (normed_image, power_image)
```

```python
import functools

import jax
import jax.numpy as jnp
import numpy as np
from jax import lax
from jax.experimental import pallas as pl
from jax.experimental.pallas import tpu as pltpu
from jax.sharding import PartitionSpec as P

BLOCK = 64
PROBES = 64
HALF = BLOCK // 2
LANES = 128
MESH = pl.DeviceIdType.MESH
VMEM = pltpu.VMEM


def load_block(a_ref, group, lane):
    return a_ref[pl.ds(group * (8 * HALF) + lane, HALF, stride=8), :]


def signed_sums(col_blocks, slot_ref, a_ref, sign_ref, g_ref):
    g_ref[...] = jnp.zeros_like(g_ref)

    @pl.loop(0, a_ref.shape[0] // (8 * HALF))
    def _(group):
        terms = []
        for lane in range(8):
            slot = slot_ref[group * 8 + lane]
            i = lax.div(slot, col_blocks)
            j = slot - i * col_blocks
            terms.append((i, load_block(a_ref, group, lane) * sign_ref[pl.ds(j, 1), :]))
        for i, term in terms:
            g_ref[i] = g_ref[i] + term


def second_products(col_blocks, shard_blocks, slot_ref, a_ref, f_ref, inv_ref, p_ref):
    p_ref[...] = jnp.zeros_like(p_ref)
    inv = inv_ref[0:1, :]
    side = lax.broadcasted_iota(jnp.int32, (PROBES, LANES), 1) // BLOCK

    @pl.loop(0, a_ref.shape[0] // (8 * HALF))
    def _(group):
        terms = []
        for lane in range(8):
            slot = slot_ref[group * 8 + lane]
            i = lax.div(slot, col_blocks)
            j = slot - i * col_blocks
            shard = lax.div(j, shard_blocks)
            j = j - shard * shard_blocks
            pair = lax.div(j, 2)
            odd = j - 2 * pair
            a = pltpu.roll(load_block(a_ref, group, lane), odd * BLOCK, axis=1)
            n = f_ref[i] * inv
            ah = a.astype(jnp.bfloat16)
            al = (a - ah.astype(jnp.float32)).astype(jnp.bfloat16)
            nh = n.astype(jnp.bfloat16)
            nl = (n - nh.astype(jnp.float32)).astype(jnp.bfloat16)
            q = lax.dot_general(
                jnp.concatenate([nh, nl, nh], axis=0),
                jnp.concatenate([ah, ah, al], axis=0),
                (((0,), (0,)), ((), ())),
                preferred_element_type=jnp.float32,
            )
            r = q[:PROBES] + pltpu.roll(q[PROBES:], BLOCK, axis=1)
            terms.append((shard, pair, jnp.where(side == odd, r, 0.0)))
        for shard, pair, term in terms:
            where = pl.ds(pl.multiple_of(pair * LANES, LANES), LANES)
            p_ref[shard, :, where] = p_ref[shard, :, where] + term


def row_exchange(
    n_row, n_col, total_rows, g_ref, had_ref, fall_ref, normed_ref, inv_ref,
    recv, natural, cs_own, cs_mid, cs_row, cs_col,
    rs_send, rs_recv, ag_send, ag_recv, cr_send, cr_recv, cc_send, cc_recv,
):
    me = lax.axis_index("row")
    me_col = lax.axis_index("col")
    bits = n_row.bit_length() - 1
    rows = g_ref.shape[1]
    part = rows // 2
    orders = [list(range(bits)), [0] + list(range(bits - 1, 0, -1))]
    base = [sum(n_row >> (s + 1) for s in range(t)) for t in range(bits + 1)]

    barrier = pltpu.get_barrier_semaphore()
    for k in range(1, n_row):
        pl.semaphore_signal(barrier, inc=1, device_id=(me ^ k, me_col), device_id_type=MESH)
    for k in range(1, n_col):
        pl.semaphore_signal(barrier, inc=1, device_id=(me, me_col ^ k), device_id_type=MESH)
    pl.semaphore_wait(barrier, n_row + n_col - 2)

    def kept(h, s, m):
        left = orders[h][s + 1 :]
        mask = 0
        for pos, bit in enumerate(left):
            if not (m >> (len(left) - 1 - pos)) & 1:
                mask |= 1 << bit
        return mask

    def rs_copy(h, s, m):
        mask = kept(h, s, m) | (1 << orders[h][s])
        slot = base[s] + m
        if s == 0:
            source = g_ref.at[me ^ mask, pl.ds(h * part, part)]
        else:
            source = recv.at[h, base[s - 1] + m]
        return pltpu.make_async_remote_copy(
            src_ref=source,
            dst_ref=recv.at[h, slot],
            send_sem=rs_send.at[h, slot],
            recv_sem=rs_recv.at[h, slot],
            device_id=(me ^ (1 << orders[h][s]), me_col),
            device_id_type=MESH,
        )

    def take(h, s, m):
        rs_copy(h, s, m).wait_recv()
        if s == 0:
            mine = g_ref[me ^ kept(h, s, m), pl.ds(h * part, part)]
        else:
            mine = recv[h, base[s - 1] + (n_row >> (s + 1)) + m]
        recv[h, base[s] + m] = recv[h, base[s] + m] + mine

    for m in range(n_row // 2):
        for h in range(2):
            rs_copy(h, 0, m).start()
    for s in range(1, bits):
        count = n_row >> (s + 1)
        for m in range(count):
            for h in range(2):
                take(h, s - 1, m)
                rs_copy(h, s, m).start()
        for m in range(count):
            for h in range(2):
                take(h, s - 1, count + m)

    def held(h, u):
        masks = [0]
        for v in range(u):
            bit = 1 << orders[h][bits - 1 - v]
            masks = masks + [x | bit for x in masks]
        return masks

    def ag_copy(h, u, m):
        mask = held(h, u)[m]
        slot = (1 << u) - 1 + m
        where = fall_ref.at[me ^ mask, pl.ds(h * part, part)]
        return pltpu.make_async_remote_copy(
            src_ref=where,
            dst_ref=where,
            send_sem=ag_send.at[h, slot],
            recv_sem=ag_recv.at[h, slot],
            device_id=(me ^ (1 << orders[h][bits - 1 - u]), me_col),
            device_id_type=MESH,
        )

    cs_own[...] = jnp.zeros_like(cs_own)
    for h in range(2):
        take(h, bits - 1, 0)
        span = pl.ds(h * part, part)
        f = jnp.dot(
            recv[h, base[bits - 1]], had_ref[...],
            precision=lax.Precision.HIGHEST, preferred_element_type=jnp.float32,
        )
        fall_ref[me, span] = f
        for u in range(bits):
            ag_copy(h, u, 0).start()
        cs_own[...] += jnp.sum((f * f).reshape(part // 8, 8, LANES), axis=0)

    def cr_copy(k):
        return pltpu.make_async_remote_copy(
            src_ref=cs_own, dst_ref=cs_row.at[k], send_sem=cr_send.at[k], recv_sem=cr_recv.at[k],
            device_id=(me ^ k, me_col), device_id_type=MESH,
        )

    def cc_copy(k):
        return pltpu.make_async_remote_copy(
            src_ref=cs_mid, dst_ref=cs_col.at[k], send_sem=cc_send.at[k], recv_sem=cc_recv.at[k],
            device_id=(me, me_col ^ k), device_id_type=MESH,
        )

    for k in range(1, n_row):
        cr_copy(k).start()
    total = cs_own[...]
    for k in range(1, n_row):
        cr_copy(k).wait_recv()
        total = total + cs_row[k]
    cs_mid[...] = total
    for k in range(1, n_col):
        cc_copy(k).start()

    def arrived(h, u, m):
        ag_copy(h, u, m).wait_recv()
        got = held(h, u)[m] | (1 << orders[h][bits - 1 - u])
        for v in range(u + 1, bits):
            ag_copy(h, v, held(h, v).index(got)).start()

    for h in range(2):
        arrived(h, 0, 0)

    for k in range(1, n_col):
        cc_copy(k).wait_recv()
        total = total + cs_col[k]
    total = jnp.broadcast_to(jnp.sum(total, axis=0, keepdims=True), (8, LANES))
    total = total + pltpu.roll(total, BLOCK, axis=1)
    root = jnp.sqrt(total / total_rows + 1e-06)
    inv_ref[...] = 1.0 / root
    normed = fall_ref[me] / root[0:1, :]
    for side in range(2):
        natural[pl.ds(side, rows, stride=2), 0:BLOCK] = normed[:, side * BLOCK : (side + 1) * BLOCK]
    for t in range(0, 2 * rows, LANES):
        stop = min(t + LANES, 2 * rows)
        normed_ref[:, t:stop] = natural[t:stop, :].T[:PROBES]

    for u in range(1, bits):
        for m in range(1 << u):
            for h in range(2):
                arrived(h, u, m)

    for h in range(2):
        for s in range(bits):
            for m in range(n_row >> (s + 1)):
                rs_copy(h, s, m).wait_send()
        for u in range(bits):
            for m in range(1 << u):
                ag_copy(h, u, m).wait_send()
    for k in range(1, n_row):
        cr_copy(k).wait_send()
    for k in range(1, n_col):
        cc_copy(k).wait_send()


def col_reduce(n_col, p_ref, out_ref, recv, send_sem, recv_sem):
    me_row = lax.axis_index("row")
    me = lax.axis_index("col")
    width = out_ref.shape[1]

    barrier = pltpu.get_barrier_semaphore()

    @pl.when(me > 0)
    def _():
        pl.semaphore_signal(barrier, inc=1, device_id=(me_row, me - 1), device_id_type=MESH)

    @pl.when(me < n_col - 1)
    def _():
        pl.semaphore_signal(barrier, inc=1, device_id=(me_row, me + 1), device_id_type=MESH)

    pl.semaphore_wait(barrier, jnp.where(me == 0, 0, 1) + jnp.where(me == n_col - 1, 0, 1))

    def copy(way, d, own=False):
        return pltpu.make_async_remote_copy(
            src_ref=p_ref.at[d] if own else recv.at[way, d],
            dst_ref=recv.at[way, d],
            send_sem=send_sem.at[way, d],
            recv_sem=recv_sem.at[way, d],
            device_id=(me_row, me + 1 if way == 0 else me - 1),
            device_id_type=MESH,
        )

    def add(way, d):
        copy(way, d).wait_recv()
        recv[way, d] = recv[way, d] + p_ref[d]

    def step(way, d):
        first = 0 if way == 0 else n_col - 1

        @pl.when((me < d) if way == 0 else (me > d))
        def _():
            @pl.when(me != first)
            def _():
                add(way, d)
                copy(way, d).start()

            @pl.when(me == first)
            def _():
                copy(way, d, own=True).start()

    for t in range(n_col - 1):
        step(0, n_col - 1 - t)
        step(1, t)

    for d in range(n_col):

        @pl.when(me == d)
        def _():
            total = p_ref[d]
            if d > 0:
                copy(0, d).wait_recv()
                total = total + recv[0, d]
            if d < n_col - 1:
                copy(1, d).wait_recv()
                total = total + recv[1, d]
            out_ref[...] = total[:, :width]

    for d in range(n_col):

        @pl.when(me < d)
        def _():
            copy(0, d).wait_send()

        @pl.when(me > d)
        def _():
            copy(1, d).wait_send()


def vmem():
    return pl.BlockSpec(memory_space=VMEM)


def local(n_row, n_col, blocks, block_slot, sign_vec):
    local_rows = sign_vec.shape[0]
    total_rows = local_rows * n_row * n_col
    row_blocks = total_rows // n_col // BLOCK
    col_blocks = total_rows // n_row // BLOCK
    count = block_slot.shape[2]
    f32 = jnp.float32
    params = functools.partial(pltpu.CompilerParams, vmem_limit_bytes=48 * 1024 * 1024)

    tiles = blocks.reshape(count // 8, 8, HALF, LANES).transpose(0, 2, 1, 3).reshape(count * HALF, LANES)
    slots = block_slot.reshape(count)
    signs = lax.all_gather(sign_vec, "col", axis=0, tiled=True).astype(f32).reshape(col_blocks, BLOCK)
    signs = jnp.concatenate([signs, signs], axis=1)

    ids = np.arange(BLOCK)
    had = np.array([[1 - 2 * (bin(k & p).count("1") % 2) for p in ids] for k in ids], np.float32)
    had = jnp.asarray(np.kron(np.eye(2, dtype=np.float32), had))

    g = pl.pallas_call(
        functools.partial(signed_sums, col_blocks),
        out_shape=jax.ShapeDtypeStruct((row_blocks, HALF, LANES), f32),
        in_specs=[pl.BlockSpec(memory_space=pltpu.SMEM), vmem(), vmem()],
        out_specs=vmem(),
        compiler_params=params(),
        name="signed_sums",
    )(slots, tiles, signs)

    rows = local_rows // 2
    dma = pltpu.SemaphoreType.DMA
    fall, normed, inv = pl.pallas_call(
        functools.partial(row_exchange, n_row, n_col, float(total_rows)),
        out_shape=(
            jax.ShapeDtypeStruct((n_row, rows, LANES), f32),
            jax.ShapeDtypeStruct((PROBES, local_rows), f32),
            jax.ShapeDtypeStruct((8, LANES), f32),
        ),
        in_specs=[vmem(), vmem()],
        out_specs=(vmem(), vmem(), vmem()),
        scratch_shapes=[
            VMEM((2, n_row - 1, rows // 2, LANES), f32),
            VMEM((local_rows, LANES), f32),
            VMEM((8, LANES), f32),
            VMEM((8, LANES), f32),
            VMEM((n_row, 8, LANES), f32),
            VMEM((n_col, 8, LANES), f32),
            dma((2, n_row - 1)),
            dma((2, n_row - 1)),
            dma((2, n_row - 1)),
            dma((2, n_row - 1)),
            dma((n_row,)),
            dma((n_row,)),
            dma((n_col,)),
            dma((n_col,)),
        ],
        compiler_params=params(collective_id=0, has_side_effects=True),
        name="row_exchange",
    )(g.reshape(n_row, rows, LANES), had)

    width = -(-local_rows // LANES) * LANES
    second = pl.pallas_call(
        functools.partial(second_products, col_blocks, local_rows // BLOCK),
        out_shape=jax.ShapeDtypeStruct((n_col, PROBES, width), f32),
        in_specs=[pl.BlockSpec(memory_space=pltpu.SMEM), vmem(), vmem(), vmem()],
        out_specs=vmem(),
        compiler_params=params(),
        name="second_products",
    )(slots, tiles, fall.reshape(row_blocks, HALF, LANES), inv)

    power = pl.pallas_call(
        functools.partial(col_reduce, n_col),
        out_shape=jax.ShapeDtypeStruct((PROBES, local_rows), f32),
        in_specs=[vmem()],
        out_specs=vmem(),
        scratch_shapes=[
            VMEM((2, n_col, PROBES, width), f32),
            dma((2, n_col)),
            dma((2, n_col)),
        ],
        compiler_params=params(collective_id=1, has_side_effects=True),
        name="col_reduce",
    )(second)
    return normed.T, power.T


def solution(mesh):
    in_specs = (P("row", "col", None, None), P("row", "col", None), P(("col", "row")))
    out_specs = (P(("col", "row"), None), P(("col", "row"), None))
    body = functools.partial(local, mesh.shape["row"], mesh.shape["col"])
    return jax.shard_map(body, mesh=mesh, in_specs=in_specs, out_specs=out_specs, check_vma=False)
```

```python
import functools

import jax
import jax.numpy as jnp
import numpy as np
from jax import lax
from jax.experimental import pallas as pl
from jax.experimental.pallas import tpu as pltpu
from jax.sharding import PartitionSpec as P

BLOCK = 64
PROBES = 64
HALF = BLOCK // 2
LANES = 128
PART = PROBES // 2
MESH = pl.DeviceIdType.MESH
VMEM = pltpu.VMEM


def load_block(a_ref, group, lane):
    return a_ref[pl.ds(group * (8 * HALF) + lane, HALF, stride=8), :]


def gather_signs(n_col, sign_ref, out_ref, send_sem, recv_sem):
    me_row = lax.axis_index("row")
    me = lax.axis_index("col")
    barrier = pltpu.get_barrier_semaphore()
    for k in range(1, n_col):
        pl.semaphore_signal(barrier, inc=1, device_id=(me_row, me ^ k), device_id_type=MESH)
    pl.semaphore_wait(barrier, n_col - 1)
    copies = [
        pltpu.make_async_remote_copy(
            src_ref=sign_ref, dst_ref=out_ref.at[me], send_sem=send_sem.at[k], recv_sem=recv_sem.at[k],
            device_id=(me_row, me ^ k), device_id_type=MESH,
        )
        for k in range(1, n_col)
    ]
    for copy in copies:
        copy.start()
    out_ref[me] = sign_ref[...]
    for copy in copies:
        copy.wait()


def signed_sums(shard_blocks, col_blocks, slot_ref, a_ref, sign_ref, low_ref, high_ref, g_ref):
    g_ref[...] = jnp.zeros_like(g_ref)

    @pl.loop(0, a_ref.shape[0] // (8 * HALF))
    def _(group):
        terms = []
        for lane in range(8):
            slot = slot_ref[group * 8 + lane]
            i = lax.div(slot, col_blocks)
            j = slot - i * col_blocks
            shard = lax.div(j, shard_blocks)
            j = j - shard * shard_blocks
            terms.append((i, load_block(a_ref, group, lane) * sign_ref[shard, pl.ds(j, 1), :]))
        for i, term in terms:
            g_ref[i] = g_ref[i] + term

    lanes = lax.broadcasted_iota(jnp.int32, (HALF // 2, LANES), 1)
    second = lanes // PART % 2 == 1

    @pl.loop(0, g_ref.shape[0] // 8)
    def _(group):
        where = pl.ds(group * 8, 8)
        g = g_ref[where]
        first, last = g[:, : HALF // 2], g[:, HALF // 2 :]
        mine = jnp.where(second, pltpu.roll(last, PART, axis=2), first)
        other = jnp.where(second, last, pltpu.roll(first, LANES - PART, axis=2))
        low_ref[where] = mine + other
        high_ref[where] = mine - other


def second_products(col_blocks, shard_blocks, slot_ref, a_ref, f_ref, inv_ref, p_ref):
    p_ref[...] = jnp.zeros_like(p_ref)
    inv = inv_ref[0:1, :]
    side = lax.broadcasted_iota(jnp.int32, (PART, LANES), 1) // BLOCK

    @pl.loop(0, a_ref.shape[0] // (8 * HALF))
    def _(group):
        terms = []
        for lane in range(8):
            slot = slot_ref[group * 8 + lane]
            i = lax.div(slot, col_blocks)
            j = slot - i * col_blocks
            shard = lax.div(j, shard_blocks)
            j = j - shard * shard_blocks
            pair = lax.div(j, 2)
            odd = j - 2 * pair
            a = load_block(a_ref, group, lane)
            a = jnp.concatenate([a[: HALF // 2], a[HALF // 2 :]], axis=1)
            n = f_ref[i] * inv
            ah = a.astype(jnp.bfloat16)
            al = (a - ah.astype(jnp.float32)).astype(jnp.bfloat16)
            nh = n.astype(jnp.bfloat16)
            nl = (n - nh.astype(jnp.float32)).astype(jnp.bfloat16)
            q = lax.dot_general(
                jnp.concatenate([nh, nl, nh], axis=0),
                jnp.concatenate([ah, ah, al], axis=0),
                (((0,), (0,)), ((), ())),
                preferred_element_type=jnp.float32,
            )
            q0 = q[:PART, :LANES] + q[PART : 2 * PART, LANES:]
            q1 = q[2 * PART : 3 * PART, :LANES] + q[3 * PART :, LANES:]
            r = jnp.where(odd == 1, q1, q0) + pltpu.roll(jnp.where(odd == 1, q0, q1), BLOCK, axis=1)
            terms.append((shard, pair, jnp.where(side == odd, r, 0.0)))
        for shard, pair, term in terms:
            where = pl.ds(pl.multiple_of(pair * LANES, LANES), LANES)
            p_ref[shard, :, where] = p_ref[shard, :, where] + term


def line_steps(n_col, p_ref, out_ref, recv, send_sem, recv_sem):
    me_row = lax.axis_index("row")
    me = lax.axis_index("col")
    width = out_ref.shape[1]

    def copy(way, d, own=False):
        return pltpu.make_async_remote_copy(
            src_ref=p_ref.at[d] if own else recv.at[way, d],
            dst_ref=recv.at[way, d],
            send_sem=send_sem.at[way, d],
            recv_sem=recv_sem.at[way, d],
            device_id=(me_row, me + 1 if way == 0 else me - 1),
            device_id_type=MESH,
        )

    def begin():
        @pl.when(me == 0)
        def _():
            for d in range(n_col - 1, 0, -1):
                copy(0, d, own=True).start()

        @pl.when(me == n_col - 1)
        def _():
            for d in range(n_col - 1):
                copy(1, d, own=True).start()

    def relay(t):
        for way, d in ((0, n_col - 1 - t), (1, t)):

            @pl.when((me > 0) & (me < d) if way == 0 else (me < n_col - 1) & (me > d))
            def _():
                copy(way, d).wait_recv()
                recv[way, d] = recv[way, d] + p_ref[d]
                copy(way, d).start()

    def finish():
        for d in range(n_col):

            @pl.when(me == d)
            def _():
                total = p_ref[d]
                if d > 0:
                    copy(0, d).wait_recv()
                    total = total + recv[0, d]
                if d < n_col - 1:
                    copy(1, d).wait_recv()
                    total = total + recv[1, d]
                out_ref[...] = total[:, :width]

        for d in range(n_col):

            @pl.when(me < d)
            def _():
                copy(0, d).wait_send()

            @pl.when(me > d)
            def _():
                copy(1, d).wait_send()

    return begin, relay, finish


def row_exchange(n_row, n_col, total_rows, both, *refs):
    if both:
        g_ref, had_ref, p_ref, fall_ref, normed_ref, inv_ref, power_ref = refs[:7]
        refs = refs[7:]
        begin, relay, finish = line_steps(n_col, p_ref, power_ref, *refs[-3:])
        refs = refs[:-3]
    else:
        g_ref, had_ref, fall_ref, normed_ref, inv_ref = refs[:5]
        refs = refs[5:]
        begin, relay, finish = lambda: None, lambda t: None, lambda: None
    recv, natural, cs_own, cs_mid, cs_row, cs_col = refs[:6]
    rs_send, rs_recv, ag_send, ag_recv, cr_send, cr_recv, cc_send, cc_recv = refs[6:]
    me = lax.axis_index("row")
    me_col = lax.axis_index("col")
    bits = n_row.bit_length() - 1
    rows = g_ref.shape[1]
    part = rows // 2
    orders = [list(range(bits)), [0] + list(range(bits - 1, 0, -1))]
    base = [sum(n_row >> (s + 1) for s in range(t)) for t in range(bits + 1)]

    barrier = pltpu.get_barrier_semaphore()
    for k in range(1, n_row):
        pl.semaphore_signal(barrier, inc=1, device_id=(me ^ k, me_col), device_id_type=MESH)
    for k in range(1, n_col):
        pl.semaphore_signal(barrier, inc=1, device_id=(me, me_col ^ k), device_id_type=MESH)
    pl.semaphore_wait(barrier, n_row + n_col - 2)

    def kept(h, s, m):
        left = orders[h][s + 1 :]
        mask = 0
        for pos, bit in enumerate(left):
            if not (m >> (len(left) - 1 - pos)) & 1:
                mask |= 1 << bit
        return mask

    def rs_copy(h, s, m):
        mask = kept(h, s, m) | (1 << orders[h][s])
        slot = base[s] + m
        if s == 0:
            source = g_ref.at[me ^ mask, pl.ds(h * part, part)]
        else:
            source = recv.at[h, base[s - 1] + m]
        return pltpu.make_async_remote_copy(
            src_ref=source,
            dst_ref=recv.at[h, slot],
            send_sem=rs_send.at[h, slot],
            recv_sem=rs_recv.at[h, slot],
            device_id=(me ^ (1 << orders[h][s]), me_col),
            device_id_type=MESH,
        )

    def take(h, s, m):
        rs_copy(h, s, m).wait_recv()
        if s == 0:
            mine = g_ref[me ^ kept(h, s, m), pl.ds(h * part, part)]
        else:
            mine = recv[h, base[s - 1] + (n_row >> (s + 1)) + m]
        recv[h, base[s] + m] = recv[h, base[s] + m] + mine

    begin()
    for m in range(n_row // 2):
        for h in range(2):
            rs_copy(h, 0, m).start()
    for s in range(1, bits):
        count = n_row >> (s + 1)
        for m in range(count):
            for h in range(2):
                take(h, s - 1, m)
                rs_copy(h, s, m).start()
        for m in range(count):
            for h in range(2):
                take(h, s - 1, count + m)

    def held(h, u):
        masks = [0]
        for v in range(u):
            bit = 1 << orders[h][bits - 1 - v]
            masks = masks + [x | bit for x in masks]
        return masks

    def ag_copy(h, u, m):
        mask = held(h, u)[m]
        slot = (1 << u) - 1 + m
        where = fall_ref.at[me ^ mask, pl.ds(h * part, part)]
        return pltpu.make_async_remote_copy(
            src_ref=where,
            dst_ref=where,
            send_sem=ag_send.at[h, slot],
            recv_sem=ag_recv.at[h, slot],
            device_id=(me ^ (1 << orders[h][bits - 1 - u]), me_col),
            device_id_type=MESH,
        )

    relay(0)
    cs_own[...] = jnp.zeros_like(cs_own)
    for h in range(2):
        take(h, bits - 1, 0)
        span = pl.ds(h * part, part)
        f = jnp.dot(
            recv[h, base[bits - 1]], had_ref[...],
            precision=lax.Precision.HIGHEST, preferred_element_type=jnp.float32,
        )
        fall_ref[me, span] = f
        for u in range(bits):
            ag_copy(h, u, 0).start()
        cs_own[...] += jnp.sum((f * f).reshape(part // 8, 8, LANES), axis=0)

    def cr_copy(k):
        return pltpu.make_async_remote_copy(
            src_ref=cs_own, dst_ref=cs_row.at[k], send_sem=cr_send.at[k], recv_sem=cr_recv.at[k],
            device_id=(me ^ k, me_col), device_id_type=MESH,
        )

    def cc_copy(k):
        return pltpu.make_async_remote_copy(
            src_ref=cs_mid, dst_ref=cs_col.at[k], send_sem=cc_send.at[k], recv_sem=cc_recv.at[k],
            device_id=(me, me_col ^ k), device_id_type=MESH,
        )

    for k in range(1, n_row):
        cr_copy(k).start()
    total = cs_own[...]
    for k in range(1, n_row):
        cr_copy(k).wait_recv()
        total = total + cs_row[k]
    cs_mid[...] = total
    for k in range(1, n_col):
        cc_copy(k).start()

    def arrived(h, u, m):
        ag_copy(h, u, m).wait_recv()
        got = held(h, u)[m] | (1 << orders[h][bits - 1 - u])
        for v in range(u + 1, bits):
            ag_copy(h, v, held(h, v).index(got)).start()

    for h in range(2):
        arrived(h, 0, 0)

    for k in range(1, n_col):
        cc_copy(k).wait_recv()
        total = total + cs_col[k]
    total = jnp.broadcast_to(jnp.sum(total, axis=0, keepdims=True), (8, LANES))
    total = total + pltpu.roll(total, BLOCK, axis=1)
    total = total + pltpu.roll(total, PART, axis=1)
    root = jnp.sqrt(total / total_rows + 1e-06)
    inv_ref[...] = 1.0 / root
    normed = fall_ref[me] / root[0:1, :]
    blocks = rows // (HALF // 2)
    for h in range(2):
        for u in range(2):
            lane = (2 * h + u) * PART
            piece = normed[:, lane : lane + PART].reshape(blocks, HALF // 2, PART)
            for i in range(blocks):
                natural[pl.ds(i * BLOCK + u * HALF + h, HALF // 2, stride=2), 0:PART] = piece[i]
    for t in range(0, blocks * BLOCK, LANES):
        stop = min(t + LANES, blocks * BLOCK)
        normed_ref[:, t:stop] = natural[t:stop, :].T[:PART]

    for t in range(1, n_col - 1):
        relay(t)
    for u in range(1, bits):
        for m in range(1 << u):
            for h in range(2):
                arrived(h, u, m)

    for h in range(2):
        for s in range(bits):
            for m in range(n_row >> (s + 1)):
                rs_copy(h, s, m).wait_send()
        for u in range(bits):
            for m in range(1 << u):
                ag_copy(h, u, m).wait_send()
    for k in range(1, n_row):
        cr_copy(k).wait_send()
    for k in range(1, n_col):
        cc_copy(k).wait_send()
    finish()


def col_reduce(n_col, p_ref, out_ref, recv, send_sem, recv_sem):
    me_row = lax.axis_index("row")
    me = lax.axis_index("col")
    barrier = pltpu.get_barrier_semaphore()

    @pl.when(me > 0)
    def _():
        pl.semaphore_signal(barrier, inc=1, device_id=(me_row, me - 1), device_id_type=MESH)

    @pl.when(me < n_col - 1)
    def _():
        pl.semaphore_signal(barrier, inc=1, device_id=(me_row, me + 1), device_id_type=MESH)

    pl.semaphore_wait(barrier, jnp.where(me == 0, 0, 1) + jnp.where(me == n_col - 1, 0, 1))

    begin, relay, finish = line_steps(n_col, p_ref, out_ref, recv, send_sem, recv_sem)
    begin()
    for t in range(n_col - 1):
        relay(t)
    finish()


def vmem():
    return pl.BlockSpec(memory_space=VMEM)


def local(n_row, n_col, blocks, block_slot, sign_vec):
    local_rows = sign_vec.shape[0]
    total_rows = local_rows * n_row * n_col
    row_blocks = total_rows // n_col // BLOCK
    col_blocks = total_rows // n_row // BLOCK
    count = block_slot.shape[2]
    f32 = jnp.float32
    params = functools.partial(pltpu.CompilerParams, vmem_limit_bytes=48 * 1024 * 1024)

    tiles = blocks.reshape(count // 8, 8, HALF, LANES).transpose(0, 2, 1, 3).reshape(count * HALF, LANES)
    slots = block_slot.reshape(count)
    dma = pltpu.SemaphoreType.DMA

    def comm(index, **kw):
        return params(collective_id=index, has_side_effects=True, **kw)

    shard_blocks = local_rows // BLOCK
    signs = sign_vec.astype(f32).reshape(shard_blocks, BLOCK)
    signs = pl.pallas_call(
        functools.partial(gather_signs, n_col),
        out_shape=jax.ShapeDtypeStruct((n_col, shard_blocks, LANES), f32),
        in_specs=[vmem()],
        out_specs=vmem(),
        scratch_shapes=[dma((n_col,)), dma((n_col,))],
        compiler_params=comm(0),
        name="gather_signs",
    )(jnp.concatenate([signs, signs], axis=1))

    ids = np.arange(PART)
    had = np.array([[1 - 2 * (bin(k & p).count("1") % 2) for p in ids] for k in ids], np.float32)
    had = jnp.asarray(np.kron(np.eye(4, dtype=np.float32), had))

    halves = pl.pallas_call(
        functools.partial(signed_sums, shard_blocks, col_blocks),
        out_shape=(jax.ShapeDtypeStruct((row_blocks, HALF // 2, LANES), f32),) * 2,
        in_specs=[pl.BlockSpec(memory_space=pltpu.SMEM), vmem(), vmem()],
        out_specs=(vmem(), vmem()),
        scratch_shapes=[VMEM((row_blocks, HALF, LANES), f32)],
        compiler_params=params(),
        name="signed_sums",
    )(slots, tiles, signs)

    rows = local_rows // 4
    width = -(-local_rows // LANES) * LANES
    row_scratch = [
        VMEM((2, n_row - 1, rows // 2, LANES), f32),
        VMEM((local_rows, LANES), f32),
        VMEM((8, LANES), f32),
        VMEM((8, LANES), f32),
        VMEM((n_row, 8, LANES), f32),
        VMEM((n_col, 8, LANES), f32),
        *[dma((2, n_row - 1))] * 4,
        *[dma((n_row,))] * 2,
        *[dma((n_col,))] * 2,
    ]
    line_scratch = [VMEM((2, n_col, PART, width), f32), dma((2, n_col)), dma((2, n_col))]
    own_part = jax.ShapeDtypeStruct((PART, local_rows), f32)

    normed, power = [], []
    second = None
    for half in range(2):
        both = half > 0
        outs = pl.pallas_call(
            functools.partial(row_exchange, n_row, n_col, float(total_rows), both),
            out_shape=(
                jax.ShapeDtypeStruct((n_row, rows, LANES), f32),
                own_part,
                jax.ShapeDtypeStruct((8, LANES), f32),
            )
            + (own_part,) * both,
            in_specs=[vmem()] * (2 + both),
            out_specs=(vmem(),) * (3 + both),
            scratch_shapes=row_scratch + line_scratch * both,
            compiler_params=comm(1 + half),
            name="row_exchange",
        )(halves[half].reshape(n_row, rows, LANES), had, *([second] * both))
        normed.append(outs[1])
        power.extend(outs[3:])
        second = pl.pallas_call(
            functools.partial(second_products, col_blocks, shard_blocks),
            out_shape=jax.ShapeDtypeStruct((n_col, PART, width), f32),
            in_specs=[pl.BlockSpec(memory_space=pltpu.SMEM), vmem(), vmem(), vmem()],
            out_specs=vmem(),
            compiler_params=params(),
            name="second_products",
        )(slots, tiles, outs[0].reshape(row_blocks, HALF // 2, LANES), outs[2])

    power.append(
        pl.pallas_call(
            functools.partial(col_reduce, n_col),
            out_shape=own_part,
            in_specs=[vmem()],
            out_specs=vmem(),
            scratch_shapes=line_scratch,
            compiler_params=comm(3),
            name="col_reduce",
        )(second)
    )
    return jnp.concatenate(normed, axis=0).T, jnp.concatenate(power, axis=0).T


def solution(mesh):
    in_specs = (P("row", "col", None, None), P("row", "col", None), P(("col", "row")))
    out_specs = (P(("col", "row"), None), P(("col", "row"), None))
    body = functools.partial(local, mesh.shape["row"], mesh.shape["col"])
    return jax.shard_map(body, mesh=mesh, in_specs=in_specs, out_specs=out_specs, check_vma=False)
```

```python
import functools

import jax
import jax.numpy as jnp
import numpy as np
from jax import lax
from jax.experimental import pallas as pl
from jax.experimental.pallas import tpu as pltpu
from jax.sharding import PartitionSpec as P

BLOCK = 64
PROBES = 64
HALF = BLOCK // 2
LANES = 128
MESH = pl.DeviceIdType.MESH
VMEM = pltpu.VMEM


def load_block(a_ref, group, lane):
    return a_ref[pl.ds(group * (8 * HALF) + lane, HALF, stride=8), :]


def gather_signs(n_col, sign_ref, out_ref, send_sem, recv_sem):
    me_row = lax.axis_index("row")
    me = lax.axis_index("col")
    barrier = pltpu.get_barrier_semaphore()
    for k in range(1, n_col):
        pl.semaphore_signal(barrier, inc=1, device_id=(me_row, me ^ k), device_id_type=MESH)
    pl.semaphore_wait(barrier, n_col - 1)
    copies = [
        pltpu.make_async_remote_copy(
            src_ref=sign_ref, dst_ref=out_ref.at[me], send_sem=send_sem.at[k], recv_sem=recv_sem.at[k],
            device_id=(me_row, me ^ k), device_id_type=MESH,
        )
        for k in range(1, n_col)
    ]
    for copy in copies:
        copy.start()
    out_ref[me] = sign_ref[...]
    for copy in copies:
        copy.wait()


def signed_sums(shard_blocks, col_blocks, slot_ref, a_ref, sign_ref, g_ref):
    g_ref[...] = jnp.zeros_like(g_ref)

    @pl.loop(0, a_ref.shape[0] // (8 * HALF))
    def _(group):
        terms = []
        for lane in range(8):
            slot = slot_ref[group * 8 + lane]
            i = lax.div(slot, col_blocks)
            j = slot - i * col_blocks
            shard = lax.div(j, shard_blocks)
            j = j - shard * shard_blocks
            terms.append((i, load_block(a_ref, group, lane) * sign_ref[shard, pl.ds(j, 1), :]))
        for i, term in terms:
            g_ref[i] = g_ref[i] + term


def second_products(col_blocks, shard_blocks, slot_ref, a_ref, f_ref, inv_ref, p_ref):
    p_ref[...] = jnp.zeros_like(p_ref)
    inv = inv_ref[0:1, :]
    side = lax.broadcasted_iota(jnp.int32, (PROBES, LANES), 1) // BLOCK

    @pl.loop(0, a_ref.shape[0] // (8 * HALF))
    def _(group):
        terms = []
        for lane in range(8):
            slot = slot_ref[group * 8 + lane]
            i = lax.div(slot, col_blocks)
            j = slot - i * col_blocks
            shard = lax.div(j, shard_blocks)
            j = j - shard * shard_blocks
            pair = lax.div(j, 2)
            odd = j - 2 * pair
            a = pltpu.roll(load_block(a_ref, group, lane), odd * BLOCK, axis=1)
            n = f_ref[i] * inv
            ah = a.astype(jnp.bfloat16)
            al = (a - ah.astype(jnp.float32)).astype(jnp.bfloat16)
            nh = n.astype(jnp.bfloat16)
            nl = (n - nh.astype(jnp.float32)).astype(jnp.bfloat16)
            q = lax.dot_general(
                jnp.concatenate([nh, nl, nh], axis=0),
                jnp.concatenate([ah, ah, al], axis=0),
                (((0,), (0,)), ((), ())),
                preferred_element_type=jnp.float32,
            )
            r = q[:PROBES] + pltpu.roll(q[PROBES:], BLOCK, axis=1)
            terms.append((shard, pair, jnp.where(side == odd, r, 0.0)))
        for shard, pair, term in terms:
            where = pl.ds(pl.multiple_of(pair * LANES, LANES), LANES)
            p_ref[shard, :, where] = p_ref[shard, :, where] + term


def row_exchange(
    n_row, n_col, total_rows, g_ref, had_ref, fall_ref, normed_ref, inv_ref,
    recv, natural, cs_own, cs_mid, cs_row, cs_col,
    rs_send, rs_recv, ag_send, ag_recv, cr_send, cr_recv, cc_send, cc_recv,
):
    me = lax.axis_index("row")
    me_col = lax.axis_index("col")
    bits = n_row.bit_length() - 1
    rows = g_ref.shape[1]
    part = rows // 2
    orders = [list(range(bits)), [0] + list(range(bits - 1, 0, -1))]
    base = [sum(n_row >> (s + 1) for s in range(t)) for t in range(bits + 1)]

    barrier = pltpu.get_barrier_semaphore()
    for k in range(1, n_row):
        pl.semaphore_signal(barrier, inc=1, device_id=(me ^ k, me_col), device_id_type=MESH)
    for k in range(1, n_col):
        pl.semaphore_signal(barrier, inc=1, device_id=(me, me_col ^ k), device_id_type=MESH)
    pl.semaphore_wait(barrier, n_row + n_col - 2)

    def kept(h, s, m):
        left = orders[h][s + 1 :]
        mask = 0
        for pos, bit in enumerate(left):
            if not (m >> (len(left) - 1 - pos)) & 1:
                mask |= 1 << bit
        return mask

    def rs_copy(h, s, m):
        mask = kept(h, s, m) | (1 << orders[h][s])
        slot = base[s] + m
        if s == 0:
            source = g_ref.at[me ^ mask, pl.ds(h * part, part)]
        else:
            source = recv.at[h, base[s - 1] + m]
        return pltpu.make_async_remote_copy(
            src_ref=source,
            dst_ref=recv.at[h, slot],
            send_sem=rs_send.at[h, slot],
            recv_sem=rs_recv.at[h, slot],
            device_id=(me ^ (1 << orders[h][s]), me_col),
            device_id_type=MESH,
        )

    def take(h, s, m):
        rs_copy(h, s, m).wait_recv()
        if s == 0:
            mine = g_ref[me ^ kept(h, s, m), pl.ds(h * part, part)]
        else:
            mine = recv[h, base[s - 1] + (n_row >> (s + 1)) + m]
        recv[h, base[s] + m] = recv[h, base[s] + m] + mine

    for m in range(n_row // 2):
        for h in range(2):
            rs_copy(h, 0, m).start()
    for s in range(1, bits):
        count = n_row >> (s + 1)
        for m in range(count):
            for h in range(2):
                take(h, s - 1, m)
                rs_copy(h, s, m).start()
        for m in range(count):
            for h in range(2):
                take(h, s - 1, count + m)

    def held(h, u):
        masks = [0]
        for v in range(u):
            bit = 1 << orders[h][bits - 1 - v]
            masks = masks + [x | bit for x in masks]
        return masks

    def ag_copy(h, u, m):
        mask = held(h, u)[m]
        slot = (1 << u) - 1 + m
        where = fall_ref.at[me ^ mask, pl.ds(h * part, part)]
        return pltpu.make_async_remote_copy(
            src_ref=where,
            dst_ref=where,
            send_sem=ag_send.at[h, slot],
            recv_sem=ag_recv.at[h, slot],
            device_id=(me ^ (1 << orders[h][bits - 1 - u]), me_col),
            device_id_type=MESH,
        )

    cs_own[...] = jnp.zeros_like(cs_own)
    for h in range(2):
        take(h, bits - 1, 0)
        span = pl.ds(h * part, part)
        f = jnp.dot(
            recv[h, base[bits - 1]], had_ref[...],
            precision=lax.Precision.HIGHEST, preferred_element_type=jnp.float32,
        )
        fall_ref[me, span] = f
        for u in range(bits):
            ag_copy(h, u, 0).start()
        cs_own[...] += jnp.sum((f * f).reshape(part // 8, 8, LANES), axis=0)

    def cr_copy(k):
        return pltpu.make_async_remote_copy(
            src_ref=cs_own, dst_ref=cs_row.at[k], send_sem=cr_send.at[k], recv_sem=cr_recv.at[k],
            device_id=(me ^ k, me_col), device_id_type=MESH,
        )

    def cc_copy(k):
        return pltpu.make_async_remote_copy(
            src_ref=cs_mid, dst_ref=cs_col.at[k], send_sem=cc_send.at[k], recv_sem=cc_recv.at[k],
            device_id=(me, me_col ^ k), device_id_type=MESH,
        )

    for k in range(1, n_row):
        cr_copy(k).start()
    total = cs_own[...]
    for k in range(1, n_row):
        cr_copy(k).wait_recv()
        total = total + cs_row[k]
    cs_mid[...] = total
    for k in range(1, n_col):
        cc_copy(k).start()

    def arrived(h, u, m):
        ag_copy(h, u, m).wait_recv()
        got = held(h, u)[m] | (1 << orders[h][bits - 1 - u])
        for v in range(u + 1, bits):
            ag_copy(h, v, held(h, v).index(got)).start()

    for h in range(2):
        arrived(h, 0, 0)

    for k in range(1, n_col):
        cc_copy(k).wait_recv()
        total = total + cs_col[k]
    total = jnp.broadcast_to(jnp.sum(total, axis=0, keepdims=True), (8, LANES))
    total = total + pltpu.roll(total, BLOCK, axis=1)
    root = jnp.sqrt(total / total_rows + 1e-06)
    inv_ref[...] = 1.0 / root
    normed = fall_ref[me] / root[0:1, :]
    for side in range(2):
        natural[pl.ds(side, rows, stride=2), 0:BLOCK] = normed[:, side * BLOCK : (side + 1) * BLOCK]
    for t in range(0, 2 * rows, LANES):
        stop = min(t + LANES, 2 * rows)
        normed_ref[:, t:stop] = natural[t:stop, :].T[:PROBES]

    for u in range(1, bits):
        for m in range(1 << u):
            for h in range(2):
                arrived(h, u, m)

    for h in range(2):
        for s in range(bits):
            for m in range(n_row >> (s + 1)):
                rs_copy(h, s, m).wait_send()
        for u in range(bits):
            for m in range(1 << u):
                ag_copy(h, u, m).wait_send()
    for k in range(1, n_row):
        cr_copy(k).wait_send()
    for k in range(1, n_col):
        cc_copy(k).wait_send()


def col_reduce(n_col, p_ref, out_ref, recv, send_sem, recv_sem):
    me_row = lax.axis_index("row")
    me = lax.axis_index("col")
    width = out_ref.shape[1]

    barrier = pltpu.get_barrier_semaphore()

    @pl.when(me > 0)
    def _():
        pl.semaphore_signal(barrier, inc=1, device_id=(me_row, me - 1), device_id_type=MESH)

    @pl.when(me < n_col - 1)
    def _():
        pl.semaphore_signal(barrier, inc=1, device_id=(me_row, me + 1), device_id_type=MESH)

    pl.semaphore_wait(barrier, jnp.where(me == 0, 0, 1) + jnp.where(me == n_col - 1, 0, 1))

    def copy(way, d, own=False):
        return pltpu.make_async_remote_copy(
            src_ref=p_ref.at[d] if own else recv.at[way, d],
            dst_ref=recv.at[way, d],
            send_sem=send_sem.at[way, d],
            recv_sem=recv_sem.at[way, d],
            device_id=(me_row, me + 1 if way == 0 else me - 1),
            device_id_type=MESH,
        )

    def add(way, d):
        copy(way, d).wait_recv()
        recv[way, d] = recv[way, d] + p_ref[d]

    def step(way, d):
        first = 0 if way == 0 else n_col - 1

        @pl.when((me < d) if way == 0 else (me > d))
        def _():
            @pl.when(me != first)
            def _():
                add(way, d)
                copy(way, d).start()

            @pl.when(me == first)
            def _():
                copy(way, d, own=True).start()

    for t in range(n_col - 1):
        step(0, n_col - 1 - t)
        step(1, t)

    for d in range(n_col):

        @pl.when(me == d)
        def _():
            total = p_ref[d]
            if d > 0:
                copy(0, d).wait_recv()
                total = total + recv[0, d]
            if d < n_col - 1:
                copy(1, d).wait_recv()
                total = total + recv[1, d]
            out_ref[...] = total[:, :width]

    for d in range(n_col):

        @pl.when(me < d)
        def _():
            copy(0, d).wait_send()

        @pl.when(me > d)
        def _():
            copy(1, d).wait_send()


def vmem():
    return pl.BlockSpec(memory_space=VMEM)


def local(n_row, n_col, blocks, block_slot, sign_vec):
    local_rows = sign_vec.shape[0]
    total_rows = local_rows * n_row * n_col
    row_blocks = total_rows // n_col // BLOCK
    col_blocks = total_rows // n_row // BLOCK
    count = block_slot.shape[2]
    f32 = jnp.float32
    params = functools.partial(pltpu.CompilerParams, vmem_limit_bytes=48 * 1024 * 1024)

    tiles = blocks.reshape(count // 8, 8, HALF, LANES).transpose(0, 2, 1, 3).reshape(count * HALF, LANES)
    slots = block_slot.reshape(count)
    dma = pltpu.SemaphoreType.DMA

    def comm(index, **kw):
        return params(collective_id=index, has_side_effects=True, **kw)

    shard_blocks = local_rows // BLOCK
    signs = sign_vec.astype(f32).reshape(shard_blocks, BLOCK)
    signs = pl.pallas_call(
        functools.partial(gather_signs, n_col),
        out_shape=jax.ShapeDtypeStruct((n_col, shard_blocks, LANES), f32),
        in_specs=[vmem()],
        out_specs=vmem(),
        scratch_shapes=[dma((n_col,)), dma((n_col,))],
        compiler_params=comm(0),
        name="gather_signs",
    )(jnp.concatenate([signs, signs], axis=1))

    ids = np.arange(BLOCK)
    had = np.array([[1 - 2 * (bin(k & p).count("1") % 2) for p in ids] for k in ids], np.float32)
    had = jnp.asarray(np.kron(np.eye(2, dtype=np.float32), had))

    g = pl.pallas_call(
        functools.partial(signed_sums, shard_blocks, col_blocks),
        out_shape=jax.ShapeDtypeStruct((row_blocks, HALF, LANES), f32),
        in_specs=[pl.BlockSpec(memory_space=pltpu.SMEM), vmem(), vmem()],
        out_specs=vmem(),
        compiler_params=params(),
        name="signed_sums",
    )(slots, tiles, signs)

    rows = local_rows // 2
    fall, normed, inv = pl.pallas_call(
        functools.partial(row_exchange, n_row, n_col, float(total_rows)),
        out_shape=(
            jax.ShapeDtypeStruct((n_row, rows, LANES), f32),
            jax.ShapeDtypeStruct((PROBES, local_rows), f32),
            jax.ShapeDtypeStruct((8, LANES), f32),
        ),
        in_specs=[vmem(), vmem()],
        out_specs=(vmem(), vmem(), vmem()),
        scratch_shapes=[
            VMEM((2, n_row - 1, rows // 2, LANES), f32),
            VMEM((local_rows, LANES), f32),
            VMEM((8, LANES), f32),
            VMEM((8, LANES), f32),
            VMEM((n_row, 8, LANES), f32),
            VMEM((n_col, 8, LANES), f32),
            dma((2, n_row - 1)),
            dma((2, n_row - 1)),
            dma((2, n_row - 1)),
            dma((2, n_row - 1)),
            dma((n_row,)),
            dma((n_row,)),
            dma((n_col,)),
            dma((n_col,)),
        ],
        compiler_params=comm(1),
        name="row_exchange",
    )(g.reshape(n_row, rows, LANES), had)

    width = -(-local_rows // LANES) * LANES
    second = pl.pallas_call(
        functools.partial(second_products, col_blocks, local_rows // BLOCK),
        out_shape=jax.ShapeDtypeStruct((n_col, PROBES, width), f32),
        in_specs=[pl.BlockSpec(memory_space=pltpu.SMEM), vmem(), vmem(), vmem()],
        out_specs=vmem(),
        compiler_params=params(),
        name="second_products",
    )(slots, tiles, fall.reshape(row_blocks, HALF, LANES), inv)

    power = pl.pallas_call(
        functools.partial(col_reduce, n_col),
        out_shape=jax.ShapeDtypeStruct((PROBES, local_rows), f32),
        in_specs=[vmem()],
        out_specs=vmem(),
        scratch_shapes=[
            VMEM((2, n_col, PROBES, width), f32),
            dma((2, n_col)),
            dma((2, n_col)),
        ],
        compiler_params=comm(2),
        name="col_reduce",
    )(second)
    return normed.T, power.T


def solution(mesh):
    in_specs = (P("row", "col", None, None), P("row", "col", None), P(("col", "row")))
    out_specs = (P(("col", "row"), None), P(("col", "row"), None))
    body = functools.partial(local, mesh.shape["row"], mesh.shape["col"])
    return jax.shard_map(body, mesh=mesh, in_specs=in_specs, out_specs=out_specs, check_vma=False)
```
